128 devices in a mesh: dp: 16 (over y, x_lo, core), mp: 8 (over x_hi, z).
Axes of the slice: x: 4 (x_hi: 2, x_lo: 2; x = x_hi * 2 + x_lo), y: 4, z: 4, core: 2. Of those that a mesh axis runs over, the one named last changes fastest.
Arguments:
- grads: bfloat16 [16, 4096, 8192], P('dp', None, 'mp'), may hold values from -6 to 6
- projector: bfloat16 [8192, 1024], P('mp'), may hold values from -0.0625 to 0.0625
- moment: float32 [4096, 1024], P(('dp', 'mp')), may hold values from -1.2 to 1.2
- second: float32 [4096, 1024], P(('dp', 'mp')), may hold values from 0.0001 to 0.01
Outputs:
- new_moment: float32 [4096, 1024], P(('dp', 'mp'))
- new_second: float32 [4096, 1024], P(('dp', 'mp'))
- update: bfloat16 [4096, 8192], P(None, 'mp')
The draws below stay inside these ranges and needn't reach their ends.
All inputs are finite; a program needn't handle non-finite values.
Results may differ from the reference program's by a relative error of at most 0.01.
Values may be sent and summed in bfloat16 or wider, within the bound.
A program may use at most 128 MiB of HBM per device.

```python
import math
import jax
import jax.numpy as jnp
from jax import lax

D = 8192
NC = 4096
R = 1024
ADAM_STEP = 10
N_DP = 16


def raised(values, rng, source, target, parts, factor):
    owner, partner = [(jnp.arange(values.shape[dim]) // (values.shape[dim] // parts)).reshape([-1 if axis == dim else 1 for axis in range(values.ndim)]) for dim in (source, target)]
    chosen = jax.random.permutation(rng, parts)[partner]
    strong = (owner == chosen) | (owner == (partner + parts // 2) % parts)
    return jnp.where(strong, factor * values, values)


def level_of(stream_key, dims, split, least, top_value):
    gain, own = 1.0, jax.random.fold_in(stream_key, 6)
    for position, blocks in split:
        heights = jnp.exp(jax.random.uniform(jax.random.fold_in(own, position), (blocks,), jnp.float32, least / len(split), top_value / len(split)))
        gain = gain * jnp.repeat(heights, dims[position] // blocks).reshape([-1 if axis == position else 1 for axis in range(len(dims))])
    return gain


def centred(own_key, extent, spread, most, shards=(), held_as=jnp.bfloat16):
    gain = level_of(own_key, extent, shards, -0.22, 0.18) if shards else 1.0
    drawn = jax.random.normal(own_key, extent, jnp.float32) * spread * gain
    return jnp.minimum(jnp.maximum(drawn, -most), most).astype(held_as)


def bell_draw_with(rng, shape, deviation, limit, split, heavy, kind=jnp.bfloat16):
    result = deviation * jax.random.normal(rng, shape, jnp.float32)
    if split:
        result = result * level_of(rng, shape, split, -0.22, 0.18)
    return jnp.clip(raised(result, jax.random.fold_in(rng, 3), *heavy), -limit, limit).astype(kind)


def setup_inputs(seed: int = 0) -> dict:
    key_list = jax.random.split(jax.random.key(seed), 5)
    grads = bell_draw_with(key_list[0], (N_DP, NC, D), 1.0, 6.0, ((0, 16), (2, 8)), (0, 1, 16, 2.0))
    projector = centred(key_list[1], (D, R), D ** -0.5, 0.0625, ((0, 8),))
    moment = centred(key_list[2], (NC, R), 0.2, 1.2, ((0, 128),), jnp.float32)
    second = jnp.clip(jnp.exp(math.log(0.01) - 4.6051702 * jax.random.uniform(key_list[3], (NC, R), jnp.float32) ** level_of(key_list[3], (NC, R), ((0, 128),), -0.2, 0.2)), 0.0001, 0.01)
    return {"grads": grads, "projector": projector, "moment": moment, "second": second}


def add_replica(total_sum, replica):
    return (total_sum + replica.astype(jnp.float32), None)

def reference(grads, projector, moment, second):
    summed, unused = lax.scan(add_replica, jnp.zeros((NC, D), jnp.float32), grads)
    projected = jnp.dot(summed, projector.astype(jnp.float32), precision=lax.Precision.HIGHEST)
    mean_grad = projected / N_DP
    new_moment = 0.9 * moment + 0.1 * mean_grad
    new_second = 0.999 * second + 0.001 * mean_grad * mean_grad
    first_fix = 1.0 - 0.9 ** ADAM_STEP
    second_fix = 1.0 - 0.999 ** ADAM_STEP
    direction = (new_moment / first_fix / (jnp.sqrt(new_second / second_fix) + 1e-08)).astype(jnp.bfloat16)
    update = jnp.dot(direction, projector.T, preferred_element_type=jnp.float32).astype(jnp.bfloat16)
    return (new_moment, new_second, update)
```

```python
import functools

import jax
import jax.numpy as jnp
from jax import lax
from jax.experimental import pallas as pl
from jax.experimental.pallas import tpu as pltpu
from jax.sharding import PartitionSpec as P

ADAM_STEP = 10
FIRST_FIX = 1.0 - 0.9**ADAM_STEP
SECOND_FIX = 1.0 - 0.999**ADAM_STEP
MESH = pl.DeviceIdType.MESH
PARTS = ((0, 384, (0, 2, 1)), (384, 384, (1, 2, 0)), (768, 256, (2, 1, 0)))
LO, HI = slice(0, 2), slice(2, 4)
ALL = slice(None)


def position():
    dp, mp = lax.axis_index("dp"), lax.axis_index("mp")
    x = (mp // 4) * 2 + (dp // 2) % 2
    return [x, dp // 4, mp % 4], dp % 2


def device(chip, core):
    x, y, z = chip
    return {"dp": (y * 2 + x % 2) * 2 + core, "mp": (x // 2) * 4 + z}


def adam(total, moment, second):
    mean_grad = total / 16.0
    new_moment = 0.9 * moment + 0.1 * mean_grad
    new_second = 0.999 * second + 0.001 * mean_grad * mean_grad
    direction = new_moment / FIRST_FIX / (jnp.sqrt(new_second / SECOND_FIX) + 1e-08)
    return new_moment, new_second, direction.astype(jnp.bfloat16)


def kernel(
    g_hbm, p_hbm, m_hbm, v_hbm,
    nm_out, nv_out, up_out,
    gs, gr, pv, mv, vv, part, rf, n1, n2, n3, dirs, stage,
    lsem, xs_sem, xr_sem, rs_s, rs_r, ag_s, ag_r, out_l, out_s, out_r,
):
    me, core = position()

    def shifted(axis, by):
        chip = list(me)
        chip[axis] = (me[axis] + by) % 4
        return chip

    def remote(src, dst, ssem, rsem, chip, to_core):
        return pltpu.make_async_remote_copy(
            src, dst, ssem, rsem, device_id=device(chip, to_core), device_id_type=MESH
        )

    def at(axes, first, third, second, block=slice(None)):
        idx = [None, None, None]
        idx[axes[0]], idx[axes[1]], idx[axes[2]] = first, second, third
        return tuple(idx)

    x_order = [(me[0] + k) % 4 for k in (2, 1, 3, 0)]
    y_order = [(me[1] + k) % 4 for k in (2, 1, 3, 0)]
    blocks = [(x_order[0], y) for y in y_order]
    blocks += [(x, y_order[0]) for x in x_order[1:]]
    blocks += [(x, y) for x in x_order[1:] for y in y_order[1:]]

    own_load, exchange = [], []
    load_p = pltpu.make_async_copy(p_hbm, pv, lsem.at[16])
    load_m = pltpu.make_async_copy(m_hbm, mv, lsem.at[17])
    load_v = pltpu.make_async_copy(v_hbm, vv, lsem.at[18])
    for i, (x, y) in enumerate(blocks):
        cp = pltpu.make_async_copy(g_hbm.at[y, x % 2, core, x // 2], gs.at[x, y], lsem.at[i])
        cp.start()
        own_load.append(cp)
        if i == 3:
            load_p.start()
    load_m.start()
    load_v.start()

    barrier = pltpu.get_barrier_semaphore()
    friends = [(shifted(a, k), core) for a in range(3) for k in (1, 2, 3)] + [(me, 1 - core)]
    for chip, to_core in friends:
        pl.semaphore_signal(barrier, inc=1, device_id=device(chip, to_core), device_id_type=MESH)
    pl.semaphore_wait(barrier, len(friends))

    for i, (x, y) in enumerate(blocks):
        cp = remote(
            g_hbm.at[y, x % 2, 1 - core, x // 2], gr.at[x, y], xs_sem.at[i], xr_sem.at[i], me, 1 - core
        )
        cp.start()
        exchange.append(cp)

    def pair_sum(i):
        x, y = blocks[i]
        own_load[i].wait()
        exchange[i].wait_recv()

        @pl.loop(0, 4)
        def _(z):
            gs[x, y, z] = gs[x, y, z] + gr[x, y, z]

    def project(p, k):
        c0, w, axes = PARTS[p]
        idx = [ALL, ALL, ALL]
        idx[axes[0]] = (me[axes[0]] + k) % 4
        rows = gs[tuple(idx)].reshape(512, 1024)
        out = jnp.dot(rows, pv[:, c0 : c0 + w], preferred_element_type=jnp.float32)
        part[tuple(idx) + (ALL, slice(c0, c0 + w))] = out.astype(jnp.bfloat16).reshape(4, 4, 32, w)

    waits = []
    count = [0, 0]

    def rs_send(src, dst, p, axis, by):
        k = count[0]
        count[0] += 1
        cp = remote(src, dst, rs_s.at[k], rs_r.at[k], shifted(axis, by), core)
        cp.start()
        waits.append(cp)
        return cp

    def ag_send(ref_at, axis, by):
        k = count[1]
        count[1] += 1
        cp = remote(dirs.at[ref_at], dirs.at[ref_at], ag_s.at[k], ag_r.at[k], shifted(axis, by), core)
        cp.start()
        waits.append(cp)
        return cp

    def cols(p):
        return pl.ds(PARTS[p][0], PARTS[p][1])

    def vcols(p):
        return slice(PARTS[p][0], PARTS[p][0] + PARTS[p][1])

    def pos(p, k):
        return (me[PARTS[p][2][0]] + k) % 4

    def far(p):
        axes = PARTS[p][2]
        c = cols(p)
        i = at(axes, pos(p, 2), LO, ALL) + (ALL, c)
        j = at(axes, pos(p, 2), HI, ALL) + (ALL, c)
        up = rs_send(part.at[i], rf.at[0, :, :, :, c], p, axes[0], 1)
        down = rs_send(part.at[j], rf.at[1, :, :, :, c], p, axes[0], 3)
        return [up, down]

    def near_plain(p, k):
        axes = PARTS[p][2]
        c = cols(p)
        half = HI if k == 1 else LO
        i = at(axes, pos(p, k), half, ALL) + (ALL, c)
        return rs_send(part.at[i], n1.at[0 if k == 1 else 1, half, :, :, c], p, axes[0], k)

    def near_relay(p, k, arrived):
        axes = PARTS[p][2]
        c, vc = cols(p), vcols(p)
        half = LO if k == 1 else HI
        slot = 0 if k == 1 else 1
        first = pos(p, k)
        arrived.wait_recv()

        @pl.loop(0, 8)
        def _(i):
            t, s = i // 4, i % 4
            a = at(axes, first, t + half.start, s)
            mine = part[a + (ALL, vc)].astype(jnp.float32)
            part[a + (ALL, vc)] = (mine + rf[slot, t, s, :, vc].astype(jnp.float32)).astype(jnp.bfloat16)

        i = at(axes, first, half, ALL) + (ALL, c)
        return rs_send(part.at[i], n1.at[slot, half, :, :, c], p, axes[0], k)

    f32 = lambda v: v.astype(jnp.float32)

    def second_stage(p, arrived):
        axes = PARTS[p][2]
        c, vc = cols(p), vcols(p)
        for cp in arrived:
            cp.wait_recv()

        @pl.loop(0, 16)
        def _(i):
            t, s = i // 4, i % 4
            a = at(axes, me[axes[0]], t, s) + (ALL, vc)
            part[a] = (f32(part[a]) + f32(n1[0, t, s, :, vc]) + f32(n1[1, t, s, :, vc])).astype(jnp.bfloat16)

        out = []
        for k in (2, 1, 3):
            i = at(axes, me[axes[0]], ALL, (me[axes[1]] + k) % 4) + (ALL, c)
            out.append(rs_send(part.at[i], n2.at[k - 1, :, :, c], p, axes[1], k))
        return out

    def third_stage(p, arrived):
        axes = PARTS[p][2]
        c, vc = cols(p), vcols(p)
        for cp in arrived:
            cp.wait_recv()

        @pl.loop(0, 4)
        def _(t):
            a = at(axes, me[axes[0]], t, me[axes[1]]) + (ALL, vc)
            part[a] = (
                f32(part[a]) + f32(n2[0, t, :, vc]) + f32(n2[1, t, :, vc]) + f32(n2[2, t, :, vc])
            ).astype(jnp.bfloat16)

        out = []
        for k in (2, 1, 3):
            i = at(axes, me[axes[0]], (me[axes[2]] + k) % 4, me[axes[1]]) + (ALL, c)
            out.append(rs_send(part.at[i], n3.at[k - 1, :, c], p, axes[2], k))
        return out

    def step_and_gather(p, arrived):
        axes = PARTS[p][2]
        c, vc = cols(p), vcols(p)
        for cp in arrived:
            cp.wait_recv()
        mine = tuple(me)
        total = f32(part[mine + (ALL, vc)]) + f32(n3[0, :, vc]) + f32(n3[1, :, vc]) + f32(n3[2, :, vc])
        new_moment, new_second, direction = adam(total, mv[:, vc], vv[:, vc])
        nm_out[:, vc] = new_moment
        nv_out[:, vc] = new_second
        dirs[mine + (ALL, vc)] = direction
        return [ag_send(mine + (ALL, c), axes[2], k) for k in (2, 1, 3)]

    def gather_second(p, arrived):
        axes = PARTS[p][2]
        for cp in arrived:
            cp.wait_recv()
        i = at(axes, me[axes[0]], ALL, me[axes[1]]) + (ALL, cols(p))
        return [ag_send(i, axes[1], k) for k in (2, 1, 3)]

    def gather_first(p, arrived):
        axes = PARTS[p][2]
        for cp in arrived:
            cp.wait_recv()
        c = cols(p)
        lo = at(axes, me[axes[0]], LO, ALL) + (ALL, c)
        hi = at(axes, me[axes[0]], HI, ALL) + (ALL, c)
        up, down = ag_send(lo, axes[0], 1), ag_send(hi, axes[0], 3)
        rest = [ag_send(hi, axes[0], 1), ag_send(lo, axes[0], 3)]
        return up, down, rest

    def gather_relay(p, up, down):
        axes = PARTS[p][2]
        c = cols(p)
        up.wait_recv()
        a = ag_send(at(axes, pos(p, 3), LO, ALL) + (ALL, c), axes[0], 1)
        down.wait_recv()
        b = ag_send(at(axes, pos(p, 1), HI, ALL) + (ALL, c), axes[0], 3)
        return [a, b]

    for i in range(4):
        pair_sum(i)
    load_p.wait()
    project(0, 2)
    far_a = far(0)
    for i in range(4, 7):
        pair_sum(i)
    project(1, 2)
    far_b = far(1)
    near = [[], [], []]
    for i in range(7, 10):
        pair_sum(i)
    project(0, 1)
    near[0].append(near_plain(0, 1))
    for i in range(10, 13):
        pair_sum(i)
    project(0, 3)
    near[0].append(near_plain(0, 3))
    for i in range(13, 16):
        pair_sum(i)
    project(2, 2)
    far_c = far(2)
    project(1, 1)
    near[1].append(near_plain(1, 1))
    project(1, 3)
    near[1].append(near_plain(1, 3))
    near[0].append(near_relay(0, 1, far_a[0]))
    near[0].append(near_relay(0, 3, far_a[1]))
    project(2, 1)
    near[2].append(near_plain(2, 1))
    project(2, 3)
    near[2].append(near_plain(2, 3))
    near[1].append(near_relay(1, 1, far_b[0]))
    near[1].append(near_relay(1, 3, far_b[1]))
    project(0, 0)
    near[2].append(near_relay(2, 1, far_c[0]))
    near[2].append(near_relay(2, 3, far_c[1]))
    project(1, 0)
    project(2, 0)

    second = [second_stage(p, near[p]) for p in range(3)]
    third = [third_stage(p, second[p]) for p in range(3)]
    load_m.wait()
    load_v.wait()
    g3 = [step_and_gather(p, third[p]) for p in range(3)]
    g2 = [gather_second(p, g3[p]) for p in range(3)]
    g1 = [gather_first(p, g2[p]) for p in range(3)]
    last = [gather_relay(p, g1[p][0], g1[p][1]) for p in range(3)]
    for p in range(3):
        for cp in g1[p][2] + last[p]:
            cp.wait_recv()

    out_waits = []
    for n, x in enumerate(x_order):
        rows = dirs[x].reshape(512, 1024)
        out = lax.dot_general(rows, pv[...], (((1,), (1,)), ((), ())), preferred_element_type=jnp.float32)
        stage[n] = out.astype(jnp.bfloat16).reshape(4, 4, 32, 1024)
        there = up_out.at[:, x % 2, core, x // 2]
        a = remote(stage.at[n], there, out_s.at[n], out_r.at[n], me, 1 - core)
        a.start()
        b = pltpu.make_async_copy(stage.at[n], there, out_l.at[n])
        b.start()
        out_waits += [a, b]
    for cp in out_waits:
        cp.wait()
    for cp in exchange + waits:
        cp.wait_send()


def shards(grads, projector, moment, second):
    g = grads.reshape(4, 2, 2, 2, 4, 32, 1024)
    bf16 = jnp.bfloat16
    anywhere = pl.BlockSpec(memory_space=pl.ANY)
    vmem = pl.BlockSpec(memory_space=pltpu.VMEM)
    dma = pltpu.SemaphoreType.DMA
    new_moment, new_second, update = pl.pallas_call(
        kernel,
        out_shape=(
            jax.ShapeDtypeStruct((32, 1024), jnp.float32),
            jax.ShapeDtypeStruct((32, 1024), jnp.float32),
            jax.ShapeDtypeStruct((4, 2, 2, 2, 4, 32, 1024), bf16),
        ),
        in_specs=[anywhere] * 4,
        out_specs=(vmem, vmem, anywhere),
        scratch_shapes=[
            pltpu.VMEM((4, 4, 4, 32, 1024), bf16),
            pltpu.VMEM((4, 4, 4, 32, 1024), bf16),
            pltpu.VMEM((1024, 1024), bf16),
            pltpu.VMEM((32, 1024), jnp.float32),
            pltpu.VMEM((32, 1024), jnp.float32),
            pltpu.VMEM((4, 4, 4, 32, 1024), bf16),
            pltpu.VMEM((2, 2, 4, 32, 1024), bf16),
            pltpu.VMEM((2, 4, 4, 32, 1024), bf16),
            pltpu.VMEM((3, 4, 32, 1024), bf16),
            pltpu.VMEM((3, 32, 1024), bf16),
            pltpu.VMEM((4, 4, 4, 32, 1024), bf16),
            pltpu.VMEM((4, 4, 4, 32, 1024), bf16),
            dma((19,)), dma((16,)), dma((16,)), dma((36,)), dma((36,)), dma((36,)), dma((36,)),
            dma((4,)), dma((4,)), dma((4,)),
        ],
        compiler_params=pltpu.CompilerParams(
            collective_id=0, has_side_effects=True, vmem_limit_bytes=48 * 2**20
        ),
        cost_estimate=pl.CostEstimate(flops=9 * 10**9, bytes_accessed=2**24, transcendentals=0),
        name="galore_step",
    )(g, projector, moment, second)
    return new_moment, new_second, update.reshape(4096, 1024)


def solution(mesh):
    return jax.shard_map(
        shards,
        mesh=mesh,
        in_specs=(P("dp", None, "mp"), P("mp", None), P(("dp", "mp"), None), P(("dp", "mp"), None)),
        out_specs=(P(("dp", "mp"), None), P(("dp", "mp"), None), P(None, "mp")),
        check_vma=False,
    )
```

```python
import jax
import jax.numpy as jnp
from jax import lax
from jax.experimental import pallas as pl
from jax.experimental.pallas import tpu as pltpu
from jax.sharding import PartitionSpec as P

ADAM_STEP = 10
FIRST_FIX = 1.0 - 0.9**ADAM_STEP
SECOND_FIX = 1.0 - 0.999**ADAM_STEP
MESH = pl.DeviceIdType.MESH
PARTS = ((0, 384, (0, 1, 2)), (384, 384, (1, 2, 0)), (768, 256, (2, 0, 1)))
ALL = slice(None)
LO, HI = slice(0, 2), slice(2, 4)


def position():
    dp, mp = lax.axis_index("dp"), lax.axis_index("mp")
    x = (mp // 4) * 2 + (dp // 2) % 2
    return [x, dp // 4, mp % 4], dp % 2


def device(chip, core):
    x, y, z = chip
    return {"dp": (y * 2 + x % 2) * 2 + core, "mp": (x // 2) * 4 + z}


def adam(total, moment, second):
    mean_grad = total / 16.0
    new_moment = 0.9 * moment + 0.1 * mean_grad
    new_second = 0.999 * second + 0.001 * mean_grad * mean_grad
    direction = new_moment / FIRST_FIX / (jnp.sqrt(new_second / SECOND_FIX) + 1e-08)
    return new_moment, new_second, direction.astype(jnp.bfloat16)


def f32(v):
    return v.astype(jnp.float32)


def bf16(v):
    return v.astype(jnp.bfloat16)


def kernel(
    g_hbm, p_hbm, m_hbm, v_hbm,
    nm_out, nv_out, up_out,
    gs, gr, pv, mv, vv, part, rf, n1, n2, n3, dirs,
    lsem, xs_sem, xr_sem, rs_s, rs_r, ag_s, ag_r, out_s, out_r,
):
    me, core = position()
    sent, arrived = [], set()
    count = {"rs": 0, "ag": 0, "out": 0}
    sems = {"rs": (rs_s, rs_r), "ag": (ag_s, ag_r), "out": (out_s, out_r)}

    def chip_at(axis, by):
        chip = list(me)
        chip[axis] = (me[axis] + by) % 4
        return chip

    def send(src, dst, kind, axis, by):
        k = count[kind]
        count[kind] += 1
        chip, to_core = (me, 1 - core) if axis is None else (chip_at(axis, by), core)
        cp = pltpu.make_async_remote_copy(
            src, dst, sems[kind][0].at[k], sems[kind][1].at[k],
            device_id=device(chip, to_core), device_id_type=MESH,
        )
        cp.start()
        sent.append(cp)
        return cp

    def arrive(*copies):
        for cp in copies:
            if id(cp) not in arrived:
                arrived.add(id(cp))
                cp.wait_recv()

    def finish():
        for cp in sent:
            arrive(cp)
            cp.wait_send()
        for cp in local:
            loaded(cp)

    def loaded(cp):
        if id(cp) not in arrived:
            arrived.add(id(cp))
            cp.wait()

    blocks = [(2, 2), (2, 1), (2, 3), (2, 0), (1, 2), (3, 2), (0, 2)]
    blocks += [(x, y) for x in (1, 3, 0) for y in (1, 3, 0)]
    place = [((me[0] + x) % 4, (me[1] + y) % 4) for x, y in blocks]

    local, own = [], []

    def load(src, dst):
        cp = pltpu.make_async_copy(src, dst, lsem.at[len(local)])
        cp.start()
        local.append(cp)
        return cp

    for i, (x, y) in enumerate(blocks):
        own.append(load(g_hbm.at[place[i][1], place[i][0] % 2, core, place[i][0] // 2], gs.at[x, y]))
        if i == 3:
            load_p = load(p_hbm, pv)
    load_m, load_v = load(m_hbm, mv), load(v_hbm, vv)

    barrier = pltpu.get_barrier_semaphore()
    friends = [(chip_at(a, k), core) for a in range(3) for k in (1, 2, 3)] + [(me, 1 - core)]
    for chip, to_core in friends:
        pl.semaphore_signal(barrier, inc=1, device_id=device(chip, to_core), device_id_type=MESH)
    pl.semaphore_wait(barrier, len(friends))

    exchange = []
    for i, (x, y) in enumerate(blocks):
        cp = pltpu.make_async_remote_copy(
            g_hbm.at[place[i][1], place[i][0] % 2, 1 - core, place[i][0] // 2], gr.at[x, y],
            xs_sem.at[i], xr_sem.at[i], device_id=device(me, 1 - core), device_id_type=MESH,
        )
        cp.start()
        sent.append(cp)
        exchange.append(cp)

    def project(first, last):
        rows = []
        for i in range(first, last):
            loaded(own[i])
            arrive(exchange[i])
        for i in range(first, last):
            x, y = blocks[i]
            rows.append((gs[x, y] + gr[x, y]).reshape(128, 1024))
        out = jnp.dot(jnp.concatenate(rows, 0), pv[...], preferred_element_type=jnp.float32)
        for i in range(first, last):
            x, y = blocks[i]
            mine = bf16(out[(i - first) * 128 : (i - first + 1) * 128]).reshape(4, 32, 1024)
            for z in range(4):
                part[x, y, (z - me[2] + 4) % 4] = mine[z]

    def at(p, a1, a2, a3):
        idx = [None, None, None]
        for axis, i in zip(PARTS[p][2], (a1, a2, a3)):
            idx[axis] = i
        return tuple(idx)

    def rest(p, a2, a3):
        _, second, third = PARTS[p][2]
        return (a2, a3) if second < third else (a3, a2)

    def cols(p):
        return (ALL, slice(PARTS[p][0], PARTS[p][0] + PARTS[p][1]))

    far = [{}, {}, {}]
    near = [{LO.start: [], HI.start: []} for _ in PARTS]

    def send_far(p, g):
        axis = PARTS[p][2][0]
        up = send(part.at[at(p, 2, g, LO) + cols(p)], rf.at[(0,) + rest(p, g, LO) + cols(p)], "rs", axis, 1)
        down = send(part.at[at(p, 2, g, HI) + cols(p)], rf.at[(1,) + rest(p, g, HI) + cols(p)], "rs", axis, 3)
        far[p][g.start] = (up, down)

    def send_near(p, by, g, half):
        slot = 0 if by == 1 else 1
        cp = send(
            part.at[at(p, by, g, half) + cols(p)], n1.at[(slot,) + rest(p, g, half) + cols(p)],
            "rs", PARTS[p][2][0], by,
        )
        near[p][g.start].append(cp)

    def send_plain(p, by, g):
        send_near(p, by, g, HI if by == 1 else LO)

    def send_relay(p, g):
        for slot, by, half in ((0, 1, LO), (1, 3, HI)):
            arrive(far[p][g.start][slot])
            i = at(p, by, g, half) + cols(p)
            part[i] = bf16(f32(part[i]) + f32(rf[(slot,) + rest(p, g, half) + cols(p)]))
            send_near(p, by, g, half)

    second = [[], [], []]

    def send_second(p, g):
        arrive(*near[p][g.start])
        i = at(p, 0, g, ALL) + cols(p)
        j = rest(p, g, ALL) + cols(p)
        part[i] = bf16(f32(part[i]) + f32(n1[(0,) + j]) + f32(n1[(1,) + j]))
        for k in range(g.start, g.stop):
            if k:
                src = part.at[at(p, 0, k, ALL) + cols(p)]
                second[p].append(send(src, n2.at[(k - 1, ALL) + cols(p)], "rs", PARTS[p][2][1], k))

    third = [[], [], []]

    def send_third(p):
        arrive(*second[p])
        i = at(p, 0, 0, ALL) + cols(p)
        total = f32(part[i])
        for k in range(3):
            total = total + f32(n2[(k, ALL) + cols(p)])
        part[i] = bf16(total)
        for k in (2, 1, 3):
            src = part.at[at(p, 0, 0, k) + cols(p)]
            third[p].append(send(src, n3.at[(k - 1,) + cols(p)], "rs", PARTS[p][2][2], k))

    def gather(p, kind_axis, src_idx, dst_idx, by):
        return send(dirs.at[src_idx + cols(p)], dirs.at[dst_idx + cols(p)], "ag", kind_axis, by)

    g3, g2 = [[], [], []], [[], [], []]
    pieces = [{}, {}, {}]
    ends = [[], [], []]

    def step(p):
        arrive(*third[p])
        c = cols(p)
        total = f32(part[(0, 0, 0) + c])
        for k in range(3):
            total = total + f32(n3[(k,) + c])
        new_moment, new_second, direction = adam(total, mv[c], vv[c])
        nm_out[c] = new_moment
        nv_out[c] = new_second
        dirs[(0, 0, 0) + c] = direction
        for k in (2, 1, 3):
            g3[p].append(gather(p, PARTS[p][2][2], (0, 0, 0), at(p, 0, 0, 4 - k), k))

    def gather_piece(p, g):
        axis = PARTS[p][2][0]
        up = gather(p, axis, at(p, 0, g, ALL), at(p, 3, g, ALL), 1)
        down = gather(p, axis, at(p, 0, g, ALL), at(p, 1, g, ALL), 3)
        pieces[p][g.start] = (up, down)

    def gather_second(p):
        arrive(*g3[p])
        for k in (2, 1, 3):
            g2[p].append(gather(p, PARTS[p][2][1], at(p, 0, 0, ALL), at(p, 0, 4 - k, ALL), k))
        gather_piece(p, slice(0, 1))

    def gather_first(p):
        arrive(*g2[p])
        gather_piece(p, slice(1, 2))
        gather_piece(p, slice(2, 4))

    def gather_relay(p, g):
        axis = PARTS[p][2][0]
        up, down = pieces[p][g.start]
        arrive(up)
        ends[p].append(gather(p, axis, at(p, 3, g, LO), at(p, 2, g, LO), 1))
        arrive(down)
        ends[p].append(gather(p, axis, at(p, 1, g, HI), at(p, 2, g, HI), 3))

    def decode(rows):
        lhs = jnp.concatenate([dirs[x, y].reshape(128, 1024) for x, y in rows], 0)
        out = lax.dot_general(lhs, pv[...], (((1,), (1,)), ((), ())), preferred_element_type=jnp.float32)
        for i, (x, y) in enumerate(rows):
            mine = bf16(out[i * 128 : (i + 1) * 128]).reshape(4, 32, 1024)
            ax, ay = (me[0] + x) % 4, (me[1] + y) % 4
            for z in range(4):
                up_out[ay, ax % 2, core, ax // 2, (me[2] + z) % 4] = mine[z]
            there = up_out.at[ay, ax % 2, core, ax // 2]
            send(there, there, "out", None, 0)

    loaded(load_p)
    project(0, 4)
    send_far(0, HI)
    send_far(0, LO)
    project(4, 7)
    send_far(1, HI)
    send_far(1, LO)
    project(7, 10)
    send_plain(0, 1, HI)
    project(10, 13)
    send_plain(0, 3, HI)
    project(13, 16)
    send_far(2, HI)
    send_plain(1, 1, HI)
    send_plain(1, 3, HI)
    send_far(2, LO)
    send_relay(0, HI)
    send_plain(2, 1, HI)
    send_plain(2, 3, HI)
    send_plain(0, 1, LO)
    send_plain(0, 3, LO)
    send_relay(1, HI)
    send_plain(1, 1, LO)
    send_plain(1, 3, LO)
    send_relay(0, LO)
    send_relay(2, HI)
    send_plain(2, 1, LO)
    send_plain(2, 3, LO)
    send_relay(1, LO)
    send_relay(2, LO)
    for p in range(3):
        send_second(p, HI)
    for p in range(3):
        send_second(p, LO)
    for p in range(3):
        send_third(p)
    loaded(load_m)
    loaded(load_v)
    for p in range(3):
        step(p)
    for p in range(3):
        gather_second(p)
    for p in range(3):
        gather_first(p)
    for g in (slice(0, 1), slice(1, 2), slice(2, 4)):
        for p in range(3):
            gather_relay(p, g)
    arrive(*ends[2])
    for x in (0, 1, 3):
        decode([(x, y) for y in (0, 1, 3)])
    arrive(*ends[1])
    decode([(x, 2) for x in (0, 1, 3)])
    arrive(*ends[0])
    decode([(2, 0), (2, 1)])
    decode([(2, 2), (2, 3)])
    finish()


def write_out(nm, nv, up, nm_out, nv_out, up_out, sem):
    copies = [
        pltpu.make_async_copy(src, dst, sem.at[i])
        for i, (src, dst) in enumerate(((up, up_out), (nm, nm_out), (nv, nv_out)))
    ]
    for cp in copies:
        cp.start()
    for cp in copies:
        cp.wait()


def shards(grads, projector, moment, second):
    half = jnp.bfloat16
    full = jnp.float32
    operands = [grads.reshape(4, 2, 2, 2, 4, 32, 1024), projector, moment, second]
    operands = [pltpu.with_memory_space_constraint(v, pltpu.HBM) for v in operands]
    anywhere = pl.BlockSpec(memory_space=pl.ANY)
    vmem = pl.BlockSpec(memory_space=pltpu.VMEM)
    dma = pltpu.SemaphoreType.DMA
    results = pl.pallas_call(
        kernel,
        out_shape=(
            pltpu.VMEM((32, 1024), full),
            pltpu.VMEM((32, 1024), full),
            pltpu.VMEM((4, 2, 2, 2, 4, 32, 1024), half),
        ),
        in_specs=[pl.BlockSpec(memory_space=pltpu.HBM)] * 4,
        out_specs=(vmem, vmem, vmem),
        scratch_shapes=[
            pltpu.VMEM((4, 4, 4, 32, 1024), half),
            pltpu.VMEM((4, 4, 4, 32, 1024), half),
            pltpu.VMEM((1024, 1024), half),
            pltpu.VMEM((32, 1024), full),
            pltpu.VMEM((32, 1024), full),
            pltpu.VMEM((4, 4, 4, 32, 1024), half),
            pltpu.VMEM((2, 4, 4, 32, 1024), half),
            pltpu.VMEM((2, 4, 4, 32, 1024), half),
            pltpu.VMEM((3, 4, 32, 1024), half),
            pltpu.VMEM((3, 32, 1024), half),
            pltpu.VMEM((4, 4, 4, 32, 1024), half),
            dma((19,)), dma((16,)), dma((16,)), dma((54,)), dma((54,)), dma((54,)), dma((54,)),
            dma((16,)), dma((16,)),
        ],
        compiler_params=pltpu.CompilerParams(
            collective_id=0, has_side_effects=True, vmem_limit_bytes=44 * 2**20
        ),
        cost_estimate=pl.CostEstimate(flops=9 * 10**9, bytes_accessed=2**24, transcendentals=0),
        name="galore_step",
    )(*operands)
    new_moment, new_second, update = results
    return pl.pallas_call(
        write_out,
        out_shape=(
            jax.ShapeDtypeStruct((32, 1024), full),
            jax.ShapeDtypeStruct((32, 1024), full),
            jax.ShapeDtypeStruct((4096, 1024), half),
        ),
        in_specs=[anywhere] * 3,
        out_specs=(anywhere,) * 3,
        scratch_shapes=[dma((3,))],
        compiler_params=pltpu.CompilerParams(vmem_limit_bytes=2**20),
        name="write_out",
    )(new_moment, new_second, update.reshape(4096, 1024))


def solution(mesh):
    return jax.shard_map(
        shards,
        mesh=mesh,
        in_specs=(P("dp", None, "mp"), P("mp", None), P(("dp", "mp"), None), P(("dp", "mp"), None)),
        out_specs=(P(("dp", "mp"), None), P(("dp", "mp"), None), P(None, "mp")),
        check_vma=False,
    )
```

```python
import jax
import jax.numpy as jnp
from jax import lax
from jax.experimental import pallas as pl
from jax.experimental.pallas import tpu as pltpu
from jax.sharding import PartitionSpec as P

ADAM_STEP = 10
FIRST_FIX = 1.0 - 0.9**ADAM_STEP
SECOND_FIX = 1.0 - 0.999**ADAM_STEP
MESH = pl.DeviceIdType.MESH
PARTS = ((0, 384, (0, 1, 2)), (384, 384, (1, 2, 0)), (768, 256, (2, 0, 1)))
ALL = slice(None)
LO, HI = slice(0, 2), slice(2, 4)


def position():
    dp, mp = lax.axis_index("dp"), lax.axis_index("mp")
    x = lax.div(mp, 4) * 2 + lax.rem(lax.div(dp, 2), 2)
    return [x, lax.div(dp, 4), lax.rem(mp, 4)], lax.rem(dp, 2)


def device(chip, core):
    x, y, z = chip
    return {"dp": (y * 2 + lax.rem(x, 2)) * 2 + core, "mp": lax.div(x, 2) * 4 + z}


def adam(total, moment, second):
    mean_grad = total / 16.0
    new_moment = 0.9 * moment + 0.1 * mean_grad
    new_second = 0.999 * second + 0.001 * mean_grad * mean_grad
    direction = new_moment / FIRST_FIX / (jnp.sqrt(new_second / SECOND_FIX) + 1e-08)
    return new_moment, new_second, direction.astype(jnp.bfloat16)


def f32(v):
    return v.astype(jnp.float32)


def bf16(v):
    return v.astype(jnp.bfloat16)


def kernel(
    g_hbm, p_hbm, m_hbm, v_hbm,
    nm_out, nv_out, up_out,
    gs, gr, pv, mv, vv, part, rf, n1, n2, n3, dirs,
    lsem, xs_sem, xr_sem, rs_s, rs_r, ag_s, ag_r, out_s, out_r,
):
    me, core = position()
    sent, arrived = [], set()
    count = {"rs": 0, "ag": 0, "out": 0}
    sems = {"rs": (rs_s, rs_r), "ag": (ag_s, ag_r), "out": (out_s, out_r)}

    ahead = [[lax.rem(m + k, 4) for k in range(4)] for m in me]
    x_lo, x_hi = [lax.rem(x, 2) for x in ahead[0]], [lax.div(x, 2) for x in ahead[0]]
    z_place = [lax.rem(z + 4 - me[2], 4) for z in range(4)]
    peers = {None: device(me, 1 - core)}
    for axis in range(3):
        for by in (1, 2, 3):
            chip = list(me)
            chip[axis] = ahead[axis][by]
            peers[axis, by] = device(chip, core)

    def send(src, dst, kind, axis, by):
        k = count[kind]
        count[kind] += 1
        peer = peers[None if axis is None else (axis, by)]
        cp = pltpu.make_async_remote_copy(
            src, dst, sems[kind][0].at[k], sems[kind][1].at[k],
            device_id=peer, device_id_type=MESH,
        )
        cp.start()
        sent.append(cp)
        return cp

    def arrive(*copies):
        for cp in copies:
            if id(cp) not in arrived:
                arrived.add(id(cp))
                cp.wait_recv()

    def finish():
        for cp in sent:
            arrive(cp)
            cp.wait_send()
        for cp in local:
            loaded(cp)

    def loaded(cp):
        if id(cp) not in arrived:
            arrived.add(id(cp))
            cp.wait()

    blocks = [(2, 2), (2, 1), (2, 3), (2, 0), (1, 2), (3, 2), (0, 2)]
    blocks += [(x, y) for x in (1, 3, 0) for y in (1, 3, 0)]

    barrier = pltpu.get_barrier_semaphore()
    for peer in peers.values():
        pl.semaphore_signal(barrier, inc=1, device_id=peer, device_id_type=MESH)
    local, own = [], []

    def load(src, dst):
        cp = pltpu.make_async_copy(src, dst, lsem.at[len(local)])
        cp.start()
        local.append(cp)
        return cp

    for i, (x, y) in enumerate(blocks):
        own.append(load(g_hbm.at[ahead[1][y], x_lo[x], core, x_hi[x]], gs.at[x, y]))
        if i == 3:
            load_p = load(p_hbm, pv)
    load_m, load_v = load(m_hbm, mv), load(v_hbm, vv)

    pl.semaphore_wait(barrier, len(peers))

    exchange = []
    for i, (x, y) in enumerate(blocks):
        cp = pltpu.make_async_remote_copy(
            g_hbm.at[ahead[1][y], x_lo[x], 1 - core, x_hi[x]], gr.at[x, y],
            xs_sem.at[i], xr_sem.at[i], device_id=peers[None], device_id_type=MESH,
        )
        cp.start()
        sent.append(cp)
        exchange.append(cp)

    def project(first, last):
        rows = []
        for i in range(first, last):
            loaded(own[i])
            arrive(exchange[i])
        for i in range(first, last):
            x, y = blocks[i]
            rows.append((gs[x, y] + gr[x, y]).reshape(128, 1024))
        out = jnp.dot(jnp.concatenate(rows, 0), pv[...], preferred_element_type=jnp.float32)
        for i in range(first, last):
            x, y = blocks[i]
            mine = bf16(out[(i - first) * 128 : (i - first + 1) * 128]).reshape(4, 32, 1024)
            for z in range(4):
                part[x, y, z_place[z]] = mine[z]

    def at(p, a1, a2, a3):
        idx = [None, None, None]
        for axis, i in zip(PARTS[p][2], (a1, a2, a3)):
            idx[axis] = i
        return tuple(idx)

    def rest(p, a2, a3):
        _, second, third = PARTS[p][2]
        return (a2, a3) if second < third else (a3, a2)

    def cols(p):
        return (ALL, slice(PARTS[p][0], PARTS[p][0] + PARTS[p][1]))

    far = [{}, {}, {}]
    near = [{LO.start: [], HI.start: []} for _ in PARTS]

    def send_far(p, g):
        axis = PARTS[p][2][0]
        up = send(part.at[at(p, 2, g, LO) + cols(p)], rf.at[(0,) + rest(p, g, LO) + cols(p)], "rs", axis, 1)
        down = send(part.at[at(p, 2, g, HI) + cols(p)], rf.at[(1,) + rest(p, g, HI) + cols(p)], "rs", axis, 3)
        far[p][g.start] = (up, down)

    def send_near(p, by, g, half):
        slot = 0 if by == 1 else 1
        cp = send(
            part.at[at(p, by, g, half) + cols(p)], n1.at[(slot,) + rest(p, g, half) + cols(p)],
            "rs", PARTS[p][2][0], by,
        )
        near[p][g.start].append(cp)

    def send_plain(p, by, g):
        send_near(p, by, g, HI if by == 1 else LO)

    def send_relay(p, g):
        for slot, by, half in ((0, 1, LO), (1, 3, HI)):
            arrive(far[p][g.start][slot])
            i = at(p, by, g, half) + cols(p)
            part[i] = bf16(f32(part[i]) + f32(rf[(slot,) + rest(p, g, half) + cols(p)]))
            send_near(p, by, g, half)

    second = [[], [], []]

    def send_second(p, g):
        arrive(*near[p][g.start])
        i = at(p, 0, g, ALL) + cols(p)
        j = rest(p, g, ALL) + cols(p)
        part[i] = bf16(f32(part[i]) + f32(n1[(0,) + j]) + f32(n1[(1,) + j]))
        for k in range(g.start, g.stop):
            if k:
                src = part.at[at(p, 0, k, ALL) + cols(p)]
                second[p].append(send(src, n2.at[(k - 1, ALL) + cols(p)], "rs", PARTS[p][2][1], k))

    third = [[], [], []]

    def send_third(p):
        arrive(*second[p])
        i = at(p, 0, 0, ALL) + cols(p)
        total = f32(part[i])
        for k in range(3):
            total = total + f32(n2[(k, ALL) + cols(p)])
        part[i] = bf16(total)
        for k in (2, 1, 3):
            src = part.at[at(p, 0, 0, k) + cols(p)]
            third[p].append(send(src, n3.at[(k - 1,) + cols(p)], "rs", PARTS[p][2][2], k))

    def gather(p, kind_axis, src_idx, dst_idx, by):
        return send(dirs.at[src_idx + cols(p)], dirs.at[dst_idx + cols(p)], "ag", kind_axis, by)

    g3, g2 = [[], [], []], [[], [], []]
    pieces = [{}, {}, {}]
    ends = [[], [], []]

    def step(p):
        arrive(*third[p])
        c = cols(p)
        total = f32(part[(0, 0, 0) + c])
        for k in range(3):
            total = total + f32(n3[(k,) + c])
        new_moment, new_second, direction = adam(total, mv[c], vv[c])
        nm_out[c] = new_moment
        nv_out[c] = new_second
        dirs[(0, 0, 0) + c] = direction
        for k in (2, 1, 3):
            g3[p].append(gather(p, PARTS[p][2][2], (0, 0, 0), at(p, 0, 0, 4 - k), k))

    def gather_piece(p, g):
        axis = PARTS[p][2][0]
        up = gather(p, axis, at(p, 0, g, ALL), at(p, 3, g, ALL), 1)
        down = gather(p, axis, at(p, 0, g, ALL), at(p, 1, g, ALL), 3)
        pieces[p][g.start] = (up, down)

    def gather_second(p):
        arrive(*g3[p])
        for k in (2, 1, 3):
            g2[p].append(gather(p, PARTS[p][2][1], at(p, 0, 0, ALL), at(p, 0, 4 - k, ALL), k))
        gather_piece(p, slice(0, 1))

    def gather_first(p):
        arrive(*g2[p])
        gather_piece(p, slice(1, 4))

    def gather_relay(p, g):
        axis = PARTS[p][2][0]
        up, down = pieces[p][g.start]
        arrive(up)
        ends[p].append(gather(p, axis, at(p, 3, g, LO), at(p, 2, g, LO), 1))
        arrive(down)
        ends[p].append(gather(p, axis, at(p, 1, g, HI), at(p, 2, g, HI), 3))

    def decode(rows):
        lhs = jnp.concatenate([dirs[x, y].reshape(128, 1024) for x, y in rows], 0)
        out = lax.dot_general(lhs, pv[...], (((1,), (1,)), ((), ())), preferred_element_type=jnp.float32)
        for i, (x, y) in enumerate(rows):
            mine = bf16(out[i * 128 : (i + 1) * 128]).reshape(4, 32, 1024)
            for z in range(4):
                up_out[ahead[1][y], x_lo[x], core, x_hi[x], ahead[2][z]] = mine[z]
            there = up_out.at[ahead[1][y], x_lo[x], core, x_hi[x]]
            send(there, there, "out", None, 0)

    loaded(load_p)
    project(0, 4)
    send_far(0, HI)
    send_far(0, LO)
    project(4, 7)
    send_far(1, HI)
    send_far(1, LO)
    project(7, 10)
    send_plain(0, 1, HI)
    project(10, 13)
    send_plain(0, 3, HI)
    project(13, 16)
    send_far(2, HI)
    send_plain(1, 1, HI)
    send_plain(1, 3, HI)
    send_far(2, LO)
    send_relay(0, HI)
    send_plain(2, 1, HI)
    send_plain(2, 3, HI)
    send_plain(0, 1, LO)
    send_plain(0, 3, LO)
    send_relay(1, HI)
    send_plain(1, 1, LO)
    send_plain(1, 3, LO)
    send_relay(0, LO)
    send_relay(2, HI)
    send_plain(2, 1, LO)
    send_plain(2, 3, LO)
    send_relay(1, LO)
    send_relay(2, LO)
    for p in range(3):
        send_second(p, HI)
    for p in range(3):
        send_second(p, LO)
    for p in range(3):
        send_third(p)
    loaded(load_m)
    loaded(load_v)
    for p in range(3):
        step(p)
    for p in range(3):
        gather_second(p)
    for p in range(3):
        gather_first(p)
    for g in (slice(0, 1), slice(1, 4)):
        for p in (2, 0, 1):
            gather_relay(p, g)
    arrive(*ends[2])
    for x in (0, 1, 3):
        decode([(x, y) for y in (0, 1, 3)])
    arrive(*ends[1])
    decode([(x, 2) for x in (0, 1, 3)])
    arrive(*ends[0])
    decode([(2, 0), (2, 1)])
    decode([(2, 2), (2, 3)])
    finish()


def write_out(nm, nv, up, nm_out, nv_out, up_out, sem):
    copies = [
        pltpu.make_async_copy(src, dst, sem.at[i])
        for i, (src, dst) in enumerate(((up, up_out), (nm, nm_out), (nv, nv_out)))
    ]
    for cp in copies:
        cp.start()
    for cp in copies:
        cp.wait()


def shards(grads, projector, moment, second):
    half = jnp.bfloat16
    full = jnp.float32
    operands = [grads.reshape(4, 2, 2, 2, 4, 32, 1024), projector, moment, second]
    operands = [pltpu.with_memory_space_constraint(v, pltpu.HBM) for v in operands]
    anywhere = pl.BlockSpec(memory_space=pl.ANY)
    vmem = pl.BlockSpec(memory_space=pltpu.VMEM)
    dma = pltpu.SemaphoreType.DMA
    results = pl.pallas_call(
        kernel,
        out_shape=(
            pltpu.VMEM((32, 1024), full),
            pltpu.VMEM((32, 1024), full),
            pltpu.VMEM((4, 2, 2, 2, 4, 32, 1024), half),
        ),
        in_specs=[pl.BlockSpec(memory_space=pltpu.HBM)] * 4,
        out_specs=(vmem, vmem, vmem),
        scratch_shapes=[
            pltpu.VMEM((4, 4, 4, 32, 1024), half),
            pltpu.VMEM((4, 4, 4, 32, 1024), half),
            pltpu.VMEM((1024, 1024), half),
            pltpu.VMEM((32, 1024), full),
            pltpu.VMEM((32, 1024), full),
            pltpu.VMEM((4, 4, 4, 32, 1024), half),
            pltpu.VMEM((2, 4, 4, 32, 1024), half),
            pltpu.VMEM((2, 4, 4, 32, 1024), half),
            pltpu.VMEM((3, 4, 32, 1024), half),
            pltpu.VMEM((3, 32, 1024), half),
            pltpu.VMEM((4, 4, 4, 32, 1024), half),
            dma((19,)), dma((16,)), dma((16,)), dma((54,)), dma((54,)), dma((54,)), dma((54,)),
            dma((16,)), dma((16,)),
        ],
        compiler_params=pltpu.CompilerParams(
            collective_id=0, has_side_effects=True, vmem_limit_bytes=44 * 2**20
        ),
        cost_estimate=pl.CostEstimate(flops=9 * 10**9, bytes_accessed=2**24, transcendentals=0),
        name="galore_step",
    )(*operands)
    new_moment, new_second, update = results
    return pl.pallas_call(
        write_out,
        out_shape=(
            jax.ShapeDtypeStruct((32, 1024), full),
            jax.ShapeDtypeStruct((32, 1024), full),
            jax.ShapeDtypeStruct((4096, 1024), half),
        ),
        in_specs=[anywhere] * 3,
        out_specs=(anywhere,) * 3,
        scratch_shapes=[dma((3,))],
        compiler_params=pltpu.CompilerParams(vmem_limit_bytes=2**20),
        name="write_out",
    )(new_moment, new_second, update.reshape(4096, 1024))


def solution(mesh):
    return jax.shard_map(
        shards,
        mesh=mesh,
        in_specs=(P("dp", None, "mp"), P("mp", None), P(("dp", "mp"), None), P(("dp", "mp"), None)),
        out_specs=(P(("dp", "mp"), None), P(("dp", "mp"), None), P(None, "mp")),
        check_vma=False,
    )
```

```python
import jax
import jax.numpy as jnp
from jax import lax
from jax.experimental import pallas as pl
from jax.experimental.pallas import tpu as pltpu
from jax.sharding import PartitionSpec as P

ADAM_STEP = 10
FIRST_FIX = 1.0 - 0.9**ADAM_STEP
SECOND_FIX = 1.0 - 0.999**ADAM_STEP
MESH = pl.DeviceIdType.MESH
PARTS = ((0, 384, (0, 1, 2)), (384, 384, (1, 2, 0)), (768, 256, (2, 0, 1)))
ALL = slice(None)
LO, HI = slice(0, 2), slice(2, 4)


def position():
    dp, mp = lax.axis_index("dp"), lax.axis_index("mp")
    x = lax.div(mp, 4) * 2 + lax.rem(lax.div(dp, 2), 2)
    return [x, lax.div(dp, 4), lax.rem(mp, 4)], lax.rem(dp, 2)


def device(chip, core):
    x, y, z = chip
    return {"dp": (y * 2 + lax.rem(x, 2)) * 2 + core, "mp": lax.div(x, 2) * 4 + z}


def adam(total, moment, second):
    mean_grad = total / 16.0
    new_moment = 0.9 * moment + 0.1 * mean_grad
    new_second = 0.999 * second + 0.001 * mean_grad * mean_grad
    direction = new_moment / FIRST_FIX / (jnp.sqrt(new_second / SECOND_FIX) + 1e-08)
    return new_moment, new_second, direction.astype(jnp.bfloat16)


def f32(v):
    return v.astype(jnp.float32)


def bf16(v):
    return v.astype(jnp.bfloat16)


def kernel(
    g_hbm, p_hbm, m_hbm, v_hbm,
    nm_out, nv_out, up_out,
    gs, gr, pv, mv, vv, part, rf, n1, n2, n3, dirs,
    lsem, xs_sem, xr_sem, rs_s, rs_r, ag_s, ag_r, out_s, out_r,
):
    me, core = position()
    sent, arrived = [], set()
    count = {"rs": 0, "ag": 0, "out": 0}
    sems = {"rs": (rs_s, rs_r), "ag": (ag_s, ag_r), "out": (out_s, out_r)}

    ahead = [[lax.rem(m + k, 4) for k in range(4)] for m in me]
    x_lo, x_hi = [lax.rem(x, 2) for x in ahead[0]], [lax.div(x, 2) for x in ahead[0]]
    z_place = [lax.rem(z + 4 - me[2], 4) for z in range(4)]
    peers = {None: device(me, 1 - core)}
    for axis in range(3):
        for by in (1, 2, 3):
            chip = list(me)
            chip[axis] = ahead[axis][by]
            peers[axis, by] = device(chip, core)

    def send(src, dst, kind, axis, by):
        k = count[kind]
        count[kind] += 1
        peer = peers[None if axis is None else (axis, by)]
        cp = pltpu.make_async_remote_copy(
            src, dst, sems[kind][0].at[k], sems[kind][1].at[k],
            device_id=peer, device_id_type=MESH,
        )
        cp.start()
        sent.append(cp)
        return cp

    def arrive(*copies):
        for cp in copies:
            if id(cp) not in arrived:
                arrived.add(id(cp))
                cp.wait_recv()

    def finish():
        for cp in sent:
            arrive(cp)
            cp.wait_send()
        for cp in local:
            loaded(cp)

    def loaded(cp):
        if id(cp) not in arrived:
            arrived.add(id(cp))
            cp.wait()

    blocks = [(2, 2), (2, 3), (1, 2), (3, 2), (0, 2), (2, 1), (2, 0)]
    blocks += [(x, y) for x in (1, 3, 0) for y in (1, 3, 0)]

    barrier = pltpu.get_barrier_semaphore()
    for peer in peers.values():
        pl.semaphore_signal(barrier, inc=1, device_id=peer, device_id_type=MESH)
    local, own = [], []

    def load(src, dst):
        cp = pltpu.make_async_copy(src, dst, lsem.at[len(local)])
        cp.start()
        local.append(cp)
        return cp

    for i, (x, y) in enumerate(blocks):
        own.append(load(g_hbm.at[ahead[1][y], x_lo[x], core, x_hi[x]], gs.at[x, y]))
        if i == 1:
            load_p = load(p_hbm, pv)
    load_m, load_v = load(m_hbm, mv), load(v_hbm, vv)

    pl.semaphore_wait(barrier, len(peers))

    exchange = []
    for i, (x, y) in enumerate(blocks):
        cp = pltpu.make_async_remote_copy(
            g_hbm.at[ahead[1][y], x_lo[x], 1 - core, x_hi[x]], gr.at[x, y],
            xs_sem.at[i], xr_sem.at[i], device_id=peers[None], device_id_type=MESH,
        )
        cp.start()
        sent.append(cp)
        exchange.append(cp)

    def project(first, last):
        rows = []
        for i in range(first, last):
            loaded(own[i])
            arrive(exchange[i])
        for i in range(first, last):
            x, y = blocks[i]
            rows.append((gs[x, y] + gr[x, y]).reshape(128, 1024))
        out = jnp.dot(jnp.concatenate(rows, 0), pv[...], preferred_element_type=jnp.float32)
        for i in range(first, last):
            x, y = blocks[i]
            mine = bf16(out[(i - first) * 128 : (i - first + 1) * 128]).reshape(4, 32, 1024)
            for z in range(4):
                part[x, y, z_place[z]] = mine[z]

    def at(p, a1, a2, a3):
        idx = [None, None, None]
        for axis, i in zip(PARTS[p][2], (a1, a2, a3)):
            idx[axis] = i
        return tuple(idx)

    def rest(p, a2, a3):
        _, second, third = PARTS[p][2]
        return (a2, a3) if second < third else (a3, a2)

    def cols(p):
        return (ALL, slice(PARTS[p][0], PARTS[p][0] + PARTS[p][1]))

    far = [{}, {}, {}]
    near = [{LO.start: [], HI.start: []} for _ in PARTS]

    def send_far(p, g):
        axis = PARTS[p][2][0]
        up = send(part.at[at(p, 2, g, LO) + cols(p)], rf.at[(0,) + rest(p, g, LO) + cols(p)], "rs", axis, 1)
        down = send(part.at[at(p, 2, g, HI) + cols(p)], rf.at[(1,) + rest(p, g, HI) + cols(p)], "rs", axis, 3)
        far[p][g.start] = (up, down)

    def send_near(p, by, g, half):
        slot = 0 if by == 1 else 1
        cp = send(
            part.at[at(p, by, g, half) + cols(p)], n1.at[(slot,) + rest(p, g, half) + cols(p)],
            "rs", PARTS[p][2][0], by,
        )
        near[p][g.start].append(cp)

    def send_plain(p, by, g):
        send_near(p, by, g, HI if by == 1 else LO)

    def send_relay(p, g):
        for slot, by, half in ((0, 1, LO), (1, 3, HI)):
            arrive(far[p][g.start][slot])
            i = at(p, by, g, half) + cols(p)
            part[i] = bf16(f32(part[i]) + f32(rf[(slot,) + rest(p, g, half) + cols(p)]))
            send_near(p, by, g, half)

    second = [[], [], []]

    def send_second(p, g):
        arrive(*near[p][g.start])
        i = at(p, 0, g, ALL) + cols(p)
        j = rest(p, g, ALL) + cols(p)
        part[i] = bf16(f32(part[i]) + f32(n1[(0,) + j]) + f32(n1[(1,) + j]))
        for k in range(g.start, g.stop):
            if k:
                src = part.at[at(p, 0, k, ALL) + cols(p)]
                second[p].append(send(src, n2.at[(k - 1, ALL) + cols(p)], "rs", PARTS[p][2][1], k))

    third = [[], [], []]

    def send_third(p):
        arrive(*second[p])
        i = at(p, 0, 0, ALL) + cols(p)
        total = f32(part[i])
        for k in range(3):
            total = total + f32(n2[(k, ALL) + cols(p)])
        part[i] = bf16(total)
        for k in (2, 1, 3):
            src = part.at[at(p, 0, 0, k) + cols(p)]
            third[p].append(send(src, n3.at[(k - 1,) + cols(p)], "rs", PARTS[p][2][2], k))

    def gather(p, kind_axis, src_idx, dst_idx, by):
        return send(dirs.at[src_idx + cols(p)], dirs.at[dst_idx + cols(p)], "ag", kind_axis, by)

    g3, g2 = [[], [], []], [[], [], []]
    pieces = [{}, {}, {}]
    ends = [[], [], []]

    def step(p):
        arrive(*third[p])
        c = cols(p)
        total = f32(part[(0, 0, 0) + c])
        for k in range(3):
            total = total + f32(n3[(k,) + c])
        new_moment, new_second, direction = adam(total, mv[c], vv[c])
        nm_out[c] = new_moment
        nv_out[c] = new_second
        dirs[(0, 0, 0) + c] = direction
        for k in (2, 1, 3):
            g3[p].append(gather(p, PARTS[p][2][2], (0, 0, 0), at(p, 0, 0, 4 - k), k))

    def gather_piece(p, g):
        axis = PARTS[p][2][0]
        up = gather(p, axis, at(p, 0, g, ALL), at(p, 3, g, ALL), 1)
        down = gather(p, axis, at(p, 0, g, ALL), at(p, 1, g, ALL), 3)
        pieces[p][g.start] = (up, down)

    def gather_second(p):
        arrive(*g3[p])
        for k in (2, 1, 3):
            g2[p].append(gather(p, PARTS[p][2][1], at(p, 0, 0, ALL), at(p, 0, 4 - k, ALL), k))
        gather_piece(p, slice(0, 1))

    def gather_first(p):
        arrive(*g2[p])
        gather_piece(p, slice(1, 4))

    def gather_relay(p, g):
        axis = PARTS[p][2][0]
        up, down = pieces[p][g.start]
        arrive(up)
        ends[p].append(gather(p, axis, at(p, 3, g, LO), at(p, 2, g, LO), 1))
        arrive(down)
        ends[p].append(gather(p, axis, at(p, 1, g, HI), at(p, 2, g, HI), 3))

    def decode(rows):
        lhs = jnp.concatenate([dirs[x, y].reshape(128, 1024) for x, y in rows], 0)
        out = lax.dot_general(lhs, pv[...], (((1,), (1,)), ((), ())), preferred_element_type=jnp.float32)
        for i, (x, y) in enumerate(rows):
            mine = bf16(out[i * 128 : (i + 1) * 128]).reshape(4, 32, 1024)
            for z in range(4):
                up_out[ahead[1][y], x_lo[x], core, x_hi[x], ahead[2][z]] = mine[z]
            there = up_out.at[ahead[1][y], x_lo[x], core, x_hi[x]]
            send(there, there, "out", None, 0)

    loaded(load_p)
    project(0, 2)
    send_far(0, HI)
    project(2, 5)
    send_far(1, HI)
    send_far(1, LO)
    project(5, 7)
    send_far(0, LO)
    project(7, 10)
    send_plain(0, 1, HI)
    project(10, 13)
    send_plain(0, 3, HI)
    project(13, 16)
    send_far(2, HI)
    send_plain(1, 1, HI)
    send_plain(1, 3, HI)
    send_far(2, LO)
    send_relay(0, HI)
    send_plain(2, 1, HI)
    send_plain(2, 3, HI)
    send_relay(1, HI)
    send_plain(0, 1, LO)
    send_plain(0, 3, LO)
    send_plain(1, 1, LO)
    send_plain(1, 3, LO)
    send_relay(2, HI)
    send_relay(0, LO)
    send_plain(2, 1, LO)
    send_plain(2, 3, LO)
    send_relay(1, LO)
    send_relay(2, LO)
    send_second(0, HI)
    send_second(1, HI)
    send_second(2, HI)
    send_second(0, LO)
    send_second(1, LO)
    send_second(2, LO)
    for p in range(3):
        send_third(p)
    loaded(load_m)
    loaded(load_v)
    for p in range(3):
        step(p)
    for p in range(3):
        gather_second(p)
    for p in range(3):
        gather_first(p)
    for g in (slice(0, 1), slice(1, 4)):
        for p in (2, 0, 1):
            gather_relay(p, g)
    arrive(*ends[2])
    for x in (0, 1, 3):
        decode([(x, y) for y in (0, 1, 3)])
    arrive(*ends[0])
    decode([(2, y) for y in (0, 1, 3)])
    arrive(*ends[1])
    decode([(0, 2), (1, 2)])
    decode([(3, 2), (2, 2)])
    finish()


def write_out(nm, nv, up, nm_out, nv_out, up_out, sem):
    copies = [
        pltpu.make_async_copy(src, dst, sem.at[i])
        for i, (src, dst) in enumerate(((up, up_out), (nm, nm_out), (nv, nv_out)))
    ]
    for cp in copies:
        cp.start()
    for cp in copies:
        cp.wait()


def shards(grads, projector, moment, second):
    half = jnp.bfloat16
    full = jnp.float32
    operands = [grads.reshape(4, 2, 2, 2, 4, 32, 1024), projector, moment, second]
    operands = [pltpu.with_memory_space_constraint(v, pltpu.HBM) for v in operands]
    anywhere = pl.BlockSpec(memory_space=pl.ANY)
    vmem = pl.BlockSpec(memory_space=pltpu.VMEM)
    dma = pltpu.SemaphoreType.DMA
    results = pl.pallas_call(
        kernel,
        out_shape=(
            pltpu.VMEM((32, 1024), full),
            pltpu.VMEM((32, 1024), full),
            pltpu.VMEM((4, 2, 2, 2, 4, 32, 1024), half),
        ),
        in_specs=[pl.BlockSpec(memory_space=pltpu.HBM)] * 4,
        out_specs=(vmem, vmem, vmem),
        scratch_shapes=[
            pltpu.VMEM((4, 4, 4, 32, 1024), half),
            pltpu.VMEM((4, 4, 4, 32, 1024), half),
            pltpu.VMEM((1024, 1024), half),
            pltpu.VMEM((32, 1024), full),
            pltpu.VMEM((32, 1024), full),
            pltpu.VMEM((4, 4, 4, 32, 1024), half),
            pltpu.VMEM((2, 4, 4, 32, 1024), half),
            pltpu.VMEM((2, 4, 4, 32, 1024), half),
            pltpu.VMEM((3, 4, 32, 1024), half),
            pltpu.VMEM((3, 32, 1024), half),
            pltpu.VMEM((4, 4, 4, 32, 1024), half),
            dma((19,)), dma((16,)), dma((16,)), dma((54,)), dma((54,)), dma((54,)), dma((54,)),
            dma((16,)), dma((16,)),
        ],
        compiler_params=pltpu.CompilerParams(
            collective_id=0, has_side_effects=True, vmem_limit_bytes=44 * 2**20
        ),
        cost_estimate=pl.CostEstimate(flops=9 * 10**9, bytes_accessed=2**24, transcendentals=0),
        name="galore_step",
    )(*operands)
    new_moment, new_second, update = results
    return pl.pallas_call(
        write_out,
        out_shape=(
            jax.ShapeDtypeStruct((32, 1024), full),
            jax.ShapeDtypeStruct((32, 1024), full),
            jax.ShapeDtypeStruct((4096, 1024), half),
        ),
        in_specs=[anywhere] * 3,
        out_specs=(anywhere,) * 3,
        scratch_shapes=[dma((3,))],
        compiler_params=pltpu.CompilerParams(vmem_limit_bytes=2**20),
        name="write_out",
    )(new_moment, new_second, update.reshape(4096, 1024))


def solution(mesh):
    return jax.shard_map(
        shards,
        mesh=mesh,
        in_specs=(P("dp", None, "mp"), P("mp", None), P(("dp", "mp"), None), P(("dp", "mp"), None)),
        out_specs=(P(("dp", "mp"), None), P(("dp", "mp"), None), P(None, "mp")),
        check_vma=False,
    )
```

```python
import jax
import jax.numpy as jnp
from jax import lax
from jax.experimental import pallas as pl
from jax.experimental.pallas import tpu as pltpu
from jax.sharding import PartitionSpec as P

ADAM_STEP = 10
FIRST_FIX = 1.0 - 0.9**ADAM_STEP
SECOND_FIX = 1.0 - 0.999**ADAM_STEP
MESH = pl.DeviceIdType.MESH
PARTS = ((0, 384, (0, 1, 2)), (384, 384, (1, 2, 0)), (768, 256, (2, 0, 1)))
ALL = slice(None)
LO, HI = slice(0, 2), slice(2, 4)


def position():
    dp, mp = lax.axis_index("dp"), lax.axis_index("mp")
    x = lax.div(mp, 4) * 2 + lax.rem(lax.div(dp, 2), 2)
    return [x, lax.div(dp, 4), lax.rem(mp, 4)], lax.rem(dp, 2)


def device(chip, core):
    x, y, z = chip
    return {"dp": (y * 2 + lax.rem(x, 2)) * 2 + core, "mp": lax.div(x, 2) * 4 + z}


def adam(total, moment, second):
    mean_grad = total / 16.0
    new_moment = 0.9 * moment + 0.1 * mean_grad
    new_second = 0.999 * second + 0.001 * mean_grad * mean_grad
    direction = new_moment / FIRST_FIX / (jnp.sqrt(new_second / SECOND_FIX) + 1e-08)
    return new_moment, new_second, direction.astype(jnp.bfloat16)


def f32(v):
    return v.astype(jnp.float32)


def bf16(v):
    return v.astype(jnp.bfloat16)


def kernel(
    g_hbm, p_hbm, m_hbm, v_hbm,
    nm_out, nv_out, up_out,
    gs, gr, pv, mv, vv, part, rf, n1, n2, n3, dirs,
    lsem, xs_sem, xr_sem, rs_s, rs_r, ag_s, ag_r, out_s, out_r,
):
    me, core = position()
    sent, arrived = [], set()
    count = {"rs": 0, "ag": 0, "out": 0}
    sems = {"rs": (rs_s, rs_r), "ag": (ag_s, ag_r), "out": (out_s, out_r)}

    ahead = [[lax.rem(m + k, 4) for k in range(4)] for m in me]
    x_lo, x_hi = [lax.rem(x, 2) for x in ahead[0]], [lax.div(x, 2) for x in ahead[0]]
    z_place = [lax.rem(z + 4 - me[2], 4) for z in range(4)]
    peers = {None: device(me, 1 - core)}
    for axis in range(3):
        for by in (1, 2, 3):
            chip = list(me)
            chip[axis] = ahead[axis][by]
            peers[axis, by] = device(chip, core)

    def send(src, dst, kind, axis, by):
        k = count[kind]
        count[kind] += 1
        peer = peers[None if axis is None else (axis, by)]
        cp = pltpu.make_async_remote_copy(
            src, dst, sems[kind][0].at[k], sems[kind][1].at[k],
            device_id=peer, device_id_type=MESH,
        )
        cp.start()
        sent.append(cp)
        return cp

    def arrive(*copies):
        for cp in copies:
            if id(cp) not in arrived:
                arrived.add(id(cp))
                cp.wait_recv()

    def finish():
        for cp in sent:
            arrive(cp)
            cp.wait_send()
        for cp in local:
            loaded(cp)

    def loaded(cp):
        if id(cp) not in arrived:
            arrived.add(id(cp))
            cp.wait()

    blocks = [(2, 2), (2, 3), (1, 2), (3, 2), (0, 2), (2, 1), (2, 0)]
    blocks += [(x, y) for x in (1, 3, 0) for y in (1, 3, 0)]

    barrier = pltpu.get_barrier_semaphore()
    for peer in peers.values():
        pl.semaphore_signal(barrier, inc=1, device_id=peer, device_id_type=MESH)
    local, own = [], []

    def load(src, dst):
        cp = pltpu.make_async_copy(src, dst, lsem.at[len(local)])
        cp.start()
        local.append(cp)
        return cp

    for i, (x, y) in enumerate(blocks):
        own.append(load(g_hbm.at[ahead[1][y], x_lo[x], core, x_hi[x]], gs.at[x, y]))
        if i == 1:
            load_p = load(p_hbm, pv)
    load_m, load_v = load(m_hbm, mv), load(v_hbm, vv)

    pl.semaphore_wait(barrier, len(peers))

    exchange = []
    for i, (x, y) in enumerate(blocks):
        cp = pltpu.make_async_remote_copy(
            g_hbm.at[ahead[1][y], x_lo[x], 1 - core, x_hi[x]], gr.at[x, y],
            xs_sem.at[i], xr_sem.at[i], device_id=peers[None], device_id_type=MESH,
        )
        cp.start()
        sent.append(cp)
        exchange.append(cp)

    def project(first, last):
        rows = []
        for i in range(first, last):
            loaded(own[i])
            arrive(exchange[i])
        for i in range(first, last):
            x, y = blocks[i]
            rows.append((gs[x, y] + gr[x, y]).reshape(128, 1024))
        out = jnp.dot(jnp.concatenate(rows, 0), pv[...], preferred_element_type=jnp.float32)
        for i in range(first, last):
            x, y = blocks[i]
            mine = bf16(out[(i - first) * 128 : (i - first + 1) * 128]).reshape(4, 32, 1024)
            for z in range(4):
                part[x, y, z_place[z]] = mine[z]

    def at(p, a1, a2, a3):
        idx = [None, None, None]
        for axis, i in zip(PARTS[p][2], (a1, a2, a3)):
            idx[axis] = i
        return tuple(idx)

    def rest(p, a2, a3):
        _, second, third = PARTS[p][2]
        return (a2, a3) if second < third else (a3, a2)

    def cols(p):
        return (ALL, slice(PARTS[p][0], PARTS[p][0] + PARTS[p][1]))

    far = [{}, {}, {}]
    near = [{LO.start: [], HI.start: []} for _ in PARTS]

    def send_far(p, g):
        axis = PARTS[p][2][0]
        up = send(part.at[at(p, 2, g, LO) + cols(p)], rf.at[(0,) + rest(p, g, LO) + cols(p)], "rs", axis, 1)
        down = send(part.at[at(p, 2, g, HI) + cols(p)], rf.at[(1,) + rest(p, g, HI) + cols(p)], "rs", axis, 3)
        far[p][g.start] = (up, down)

    def send_near(p, by, g, half):
        slot = 0 if by == 1 else 1
        cp = send(
            part.at[at(p, by, g, half) + cols(p)], n1.at[(slot,) + rest(p, g, half) + cols(p)],
            "rs", PARTS[p][2][0], by,
        )
        near[p][g.start].append(cp)

    def send_plain(p, by, g):
        send_near(p, by, g, HI if by == 1 else LO)

    def send_relay(p, g):
        for slot, by, half in ((0, 1, LO), (1, 3, HI)):
            arrive(far[p][g.start][slot])
            i = at(p, by, g, half) + cols(p)
            part[i] = bf16(f32(part[i]) + f32(rf[(slot,) + rest(p, g, half) + cols(p)]))
            send_near(p, by, g, half)

    second = [[], [], []]

    def send_second(p, g):
        arrive(*near[p][g.start])
        i = at(p, 0, g, ALL) + cols(p)
        j = rest(p, g, ALL) + cols(p)
        part[i] = bf16(f32(part[i]) + f32(n1[(0,) + j]) + f32(n1[(1,) + j]))
        for k in range(g.start, g.stop):
            if k:
                src = part.at[at(p, 0, k, ALL) + cols(p)]
                second[p].append(send(src, n2.at[(k - 1, ALL) + cols(p)], "rs", PARTS[p][2][1], k))

    third = [[], [], []]

    def send_third(p):
        arrive(*second[p])
        i = at(p, 0, 0, ALL) + cols(p)
        total = f32(part[i])
        for k in range(3):
            total = total + f32(n2[(k, ALL) + cols(p)])
        part[i] = bf16(total)
        for k in (2, 1, 3):
            src = part.at[at(p, 0, 0, k) + cols(p)]
            third[p].append(send(src, n3.at[(k - 1,) + cols(p)], "rs", PARTS[p][2][2], k))

    def gather(p, kind_axis, src_idx, dst_idx, by):
        return send(dirs.at[src_idx + cols(p)], dirs.at[dst_idx + cols(p)], "ag", kind_axis, by)

    g3, g2 = [[], [], []], [[], [], []]
    pieces = [{}, {}, {}]
    ends = [[], [], []]

    def step(p):
        arrive(*third[p])
        c = cols(p)
        total = f32(part[(0, 0, 0) + c])
        for k in range(3):
            total = total + f32(n3[(k,) + c])
        new_moment, new_second, direction = adam(total, mv[c], vv[c])
        nm_out[c] = new_moment
        nv_out[c] = new_second
        dirs[(0, 0, 0) + c] = direction
        for k in (2, 1, 3):
            g3[p].append(gather(p, PARTS[p][2][2], (0, 0, 0), at(p, 0, 0, 4 - k), k))

    def gather_piece(p, g):
        axis = PARTS[p][2][0]
        if g.start == 0:
            up = gather(p, axis, at(p, 0, g, ALL), at(p, 3, g, ALL), 1)
            down = gather(p, axis, at(p, 0, g, ALL), at(p, 1, g, ALL), 3)
        else:
            up = gather(p, axis, at(p, 0, g, LO), at(p, 3, g, LO), 1)
            down = gather(p, axis, at(p, 0, g, HI), at(p, 1, g, HI), 3)
        pieces[p][g.start] = (up, down)

    others = []

    def gather_others(p, g):
        axis = PARTS[p][2][0]
        others.append(gather(p, axis, at(p, 0, g, HI), at(p, 3, g, HI), 1))
        others.append(gather(p, axis, at(p, 0, g, LO), at(p, 1, g, LO), 3))

    def gather_second(p):
        arrive(*g3[p])
        for k in (2, 1, 3):
            g2[p].append(gather(p, PARTS[p][2][1], at(p, 0, 0, ALL), at(p, 0, 4 - k, ALL), k))
        gather_piece(p, slice(0, 1))

    def gather_first(p):
        arrive(*g2[p])
        gather_piece(p, slice(1, 4))

    def gather_relay(p, g):
        axis = PARTS[p][2][0]
        up, down = pieces[p][g.start]
        arrive(up)
        ends[p].append(gather(p, axis, at(p, 3, g, LO), at(p, 2, g, LO), 1))
        arrive(down)
        ends[p].append(gather(p, axis, at(p, 1, g, HI), at(p, 2, g, HI), 3))

    def decode(rows):
        lhs = jnp.concatenate([dirs[x, y].reshape(128, 1024) for x, y in rows], 0)
        out = lax.dot_general(lhs, pv[...], (((1,), (1,)), ((), ())), preferred_element_type=jnp.float32)
        for i, (x, y) in enumerate(rows):
            mine = bf16(out[i * 128 : (i + 1) * 128]).reshape(4, 32, 1024)
            for z in range(4):
                up_out[ahead[1][y], x_lo[x], core, x_hi[x], ahead[2][z]] = mine[z]
            there = up_out.at[ahead[1][y], x_lo[x], core, x_hi[x]]
            send(there, there, "out", None, 0)

    loaded(load_p)
    project(0, 2)
    send_far(0, HI)
    project(2, 5)
    send_far(1, HI)
    send_far(1, LO)
    project(5, 7)
    send_far(0, LO)
    project(7, 10)
    send_plain(0, 1, HI)
    project(10, 13)
    send_plain(0, 3, HI)
    project(13, 16)
    send_far(2, HI)
    send_plain(1, 1, HI)
    send_plain(1, 3, HI)
    send_far(2, LO)
    send_relay(0, HI)
    send_plain(2, 1, HI)
    send_plain(2, 3, HI)
    send_relay(1, HI)
    send_plain(0, 1, LO)
    send_plain(0, 3, LO)
    send_plain(1, 1, LO)
    send_plain(1, 3, LO)
    send_relay(2, HI)
    send_relay(0, LO)
    send_plain(2, 1, LO)
    send_plain(2, 3, LO)
    send_relay(1, LO)
    send_relay(2, LO)
    send_second(0, HI)
    send_second(1, HI)
    send_second(2, HI)
    send_second(0, LO)
    send_second(1, LO)
    send_second(2, LO)
    for p in range(3):
        send_third(p)
    loaded(load_m)
    loaded(load_v)
    for p in range(3):
        step(p)
    for p in range(3):
        gather_second(p)
    for p in range(3):
        gather_first(p)
    for p in (2, 0, 1):
        gather_relay(p, slice(0, 1))
    for p in (2, 0, 1):
        gather_others(p, slice(1, 4))
    for p in (2, 0, 1):
        gather_relay(p, slice(1, 4))
    arrive(*others)
    arrive(*ends[2])
    for x in (0, 1, 3):
        decode([(x, y) for y in (0, 1, 3)])
    arrive(*ends[0])
    decode([(2, y) for y in (0, 1, 3)])
    arrive(*ends[1])
    decode([(0, 2), (1, 2)])
    decode([(3, 2), (2, 2)])
    finish()


def write_out(nm, nv, up, nm_out, nv_out, up_out, sem):
    copies = [
        pltpu.make_async_copy(src, dst, sem.at[i])
        for i, (src, dst) in enumerate(((up, up_out), (nm, nm_out), (nv, nv_out)))
    ]
    for cp in copies:
        cp.start()
    for cp in copies:
        cp.wait()


def shards(grads, projector, moment, second):
    half = jnp.bfloat16
    full = jnp.float32
    operands = [grads.reshape(4, 2, 2, 2, 4, 32, 1024), projector, moment, second]
    operands = [pltpu.with_memory_space_constraint(v, pltpu.HBM) for v in operands]
    anywhere = pl.BlockSpec(memory_space=pl.ANY)
    vmem = pl.BlockSpec(memory_space=pltpu.VMEM)
    dma = pltpu.SemaphoreType.DMA
    results = pl.pallas_call(
        kernel,
        out_shape=(
            pltpu.VMEM((32, 1024), full),
            pltpu.VMEM((32, 1024), full),
            pltpu.VMEM((4, 2, 2, 2, 4, 32, 1024), half),
        ),
        in_specs=[pl.BlockSpec(memory_space=pltpu.HBM)] * 4,
        out_specs=(vmem, vmem, vmem),
        scratch_shapes=[
            pltpu.VMEM((4, 4, 4, 32, 1024), half),
            pltpu.VMEM((4, 4, 4, 32, 1024), half),
            pltpu.VMEM((1024, 1024), half),
            pltpu.VMEM((32, 1024), full),
            pltpu.VMEM((32, 1024), full),
            pltpu.VMEM((4, 4, 4, 32, 1024), half),
            pltpu.VMEM((2, 4, 4, 32, 1024), half),
            pltpu.VMEM((2, 4, 4, 32, 1024), half),
            pltpu.VMEM((3, 4, 32, 1024), half),
            pltpu.VMEM((3, 32, 1024), half),
            pltpu.VMEM((4, 4, 4, 32, 1024), half),
            dma((19,)), dma((16,)), dma((16,)), dma((54,)), dma((54,)), dma((54,)), dma((54,)),
            dma((16,)), dma((16,)),
        ],
        compiler_params=pltpu.CompilerParams(
            collective_id=0, has_side_effects=True, vmem_limit_bytes=44 * 2**20
        ),
        cost_estimate=pl.CostEstimate(flops=9 * 10**9, bytes_accessed=2**24, transcendentals=0),
        name="galore_step",
    )(*operands)
    new_moment, new_second, update = results
    return pl.pallas_call(
        write_out,
        out_shape=(
            jax.ShapeDtypeStruct((32, 1024), full),
            jax.ShapeDtypeStruct((32, 1024), full),
            jax.ShapeDtypeStruct((4096, 1024), half),
        ),
        in_specs=[anywhere] * 3,
        out_specs=(anywhere,) * 3,
        scratch_shapes=[dma((3,))],
        compiler_params=pltpu.CompilerParams(vmem_limit_bytes=2**20),
        name="write_out",
    )(new_moment, new_second, update.reshape(4096, 1024))


def solution(mesh):
    return jax.shard_map(
        shards,
        mesh=mesh,
        in_specs=(P("dp", None, "mp"), P("mp", None), P(("dp", "mp"), None), P(("dp", "mp"), None)),
        out_specs=(P(("dp", "mp"), None), P(("dp", "mp"), None), P(None, "mp")),
        check_vma=False,
    )
```
